32 devices in a mesh: pipe: 4 (over z), expert: 8 (over y, x, core).
Axes of the slice: x: 2, y: 2, z: 4, core: 2. Of those that a mesh axis runs over, the one named last changes fastest.
Arguments:
- grad_in: bfloat16 [4, 2, 1024, 7168], P('pipe', None, 'expert'), may hold values from -0.59765625 to 0.59765625
- route: int32 [4, 2, 8, 1], P('pipe'), may hold values from 0 to 1; in each aligned block of 8 rows (0 to 7, 8 to 15, ..., all dimensions but the last counted through in order) at most 8 rows name the same one
- stored: bfloat16 [4, 2, 1024, 4096], P('pipe', None, None, 'expert'), may hold values from -6 to 6
- down_weight: bfloat16 [4, 1024, 14336], P('pipe', None, 'expert'), as said below
Outputs:
- d_stored: bfloat16 [4, 2, 1024, 4096], P('pipe', None, None, 'expert')
- weight_grad: bfloat16 [4, 512, 14336], P('pipe', None, 'expert')
The draws below stay inside these ranges and needn't reach their ends.
Inputs may be any that keep to these rules, and one draw needn't show every extreme that they name: `route`: the 1 entries of a block are different experts. In each micro-batch of each section at most 8 of the 8 blocks name one expert, and in some micro-batch one expert is named by exactly 8. `down_weight`: the copies of sections p and 3 - p are equal.
All inputs are finite; a program needn't handle non-finite values.
Results may differ from the reference program's by a relative error of at most 0.006.
Values may be sent and summed in bfloat16 or wider, within the bound.
No kernel may reach another device: no remote copies, remote signals or barrier semaphores. Data moves between devices by JAX's collectives and lax.ppermute only.
A program may use at most 128 MiB of HBM per device.

```python
import math
import jax
import jax.numpy as jnp
import numpy as np

D = 7168
FF_W = 1024
BLOCK = 128
MICRO = 2
CAP_BLOCKS = 8
EXPERTS = 2
TOP = 1
CAP_ROWS = 1024
HQ = 256
N_PIPE = 4
N_EXPERT = 8


def draw_down_weight(key, part):
    key = jax.random.fold_in(key, 7)
    first_half = jax.random.normal(key, (N_PIPE // 2, FF_W, EXPERTS * D), jnp.float32) * FF_W ** (-0.5)
    return jnp.concatenate([first_half, first_half[::-1]], axis=0).astype(jnp.bfloat16)


def steps_of(key, shape, split, smallest, top_value):
    loudness = 1.0
    for dim, blocks in split:
        heights = jax.random.uniform(jax.random.fold_in(jax.random.fold_in(key, 6), dim), (blocks,), jnp.float32, smallest / len(split), top_value / len(split))
        loudness = loudness * jnp.repeat(jnp.exp(heights), shape[dim] // blocks).reshape((-1,) + (1,) * (len(shape) - 1 - dim))
    return loudness


def routed_block(rng, own, number, rows, number_of, top, limit, lean):
    ranking = jax.random.permutation(rng, number_of)
    packed, ordinary = portions_of(number_of, rows * top, limit, lean, True), portions_of(number_of, rows * top, limit, lean, False)
    places = jnp.arange(number_of)

    def named(tallies, rotation):
        used = int((tallies > 0).sum())
        fixed = max(1, used // 4)
        passed = fixed + (places - fixed + rotation * (used - fixed)) % max(1, number_of - fixed)
        return jnp.zeros((number_of,), jnp.int32).at[ranking[jnp.where(places < fixed, places, passed)]].set(jnp.asarray(tallies, jnp.int32))

    tallies = jnp.where(number % 4 == 0, named(packed, number // 4), named(ordinary, number - number // 4 - 1))
    mixed = jax.random.permutation(jax.random.fold_in(own, 3), number_of)
    source_of, sink = mixed[0:number_of // 2 * 2:2], mixed[1:number_of // 2 * 2:2]
    room = jnp.minimum(tallies[source_of] - 1, limit - tallies[sink]) // 2
    room = jnp.where((source_of == ranking[0]) | (sink == ranking[0]) | (tallies[sink] == 0), 0, jnp.maximum(room, 0))
    passed = jax.random.randint(jax.random.fold_in(own, 4), (number_of // 2,), 0, 1 << 20) % (room + 1)
    tallies = tallies.at[source_of].add(-passed).at[sink].add(passed)
    members = jnp.searchsorted(jnp.cumsum(tallies), jnp.arange(rows * top), side="right").astype(jnp.int32)
    listing = members.reshape(top, rows).T
    listing = listing[jax.random.permutation(jax.random.fold_in(own, 1), rows)]
    rotation = jax.random.randint(jax.random.fold_in(own, 2), (rows, 1), 0, top)
    return jnp.take_along_axis(listing, (jnp.arange(top)[None, :] + rotation) % top, axis=1)


def portions_of(count, total, most, skew, full):
    portions = [(1 << 20) // math.isqrt(grade ** skew) + 1 for grade in range(1, count + 1)]
    largest = most if full else min(most, max(-(-total // count), total * portions[0] // sum(portions)))
    least = 1 if total - largest >= count - 1 else 0
    holding, rest = [largest] + [least] * (count - 1), total - largest - least * (count - 1)
    while rest > 0:
        candidates = [i for i in range(1, count) if holding[i] < largest] or [i for i in range(1, count) if holding[i] < most]
        mass, budget = sum([portions[i] for i in candidates]), rest
        for i in candidates:
            addition = min(most - holding[i], max(1, budget * portions[i] // mass), rest)
            holding[i] = holding[i] + addition
            rest = rest - addition
    return np.array(holding)


def scatter_about(stream_key, shape, spread, limit, shards=(), kind=jnp.bfloat16):
    result = jax.random.normal(stream_key, shape, jnp.float32) * spread
    if len(shards) > 0:
        result = steps_of(stream_key, shape, shards, -0.22, 0.18) * result
    return jnp.clip(result, min=-limit, max=limit).astype(kind)


def setup_inputs(seed: int = 0) -> dict:
    key_list = jax.random.split(jax.random.key(seed), 5)
    grad_in = scatter_about(key_list[0], (N_PIPE, MICRO, N_EXPERT * BLOCK, D), 0.1, 0.59765625, ((0, 4), (2, 8)))
    route_keys = jax.random.split(jax.random.fold_in(key_list[1], 1), N_PIPE * MICRO * N_EXPERT // N_EXPERT)
    route_turns = jax.random.permutation(jax.random.fold_in(key_list[1], 3), N_PIPE * MICRO * N_EXPERT // N_EXPERT)
    route = jax.vmap(lambda own, number: routed_block(jax.random.fold_in(key_list[1], 2), own, number, N_EXPERT, EXPERTS, TOP, CAP_BLOCKS, 2))(route_keys, route_turns).reshape((N_PIPE, MICRO, N_EXPERT, TOP))
    stored = scatter_about(key_list[2], (N_PIPE, MICRO, CAP_ROWS, EXPERTS * 2 * FF_W), 1.0, 6.0, ((0, 4), (3, 8)))
    down_weight = draw_down_weight(jax.random.fold_in(key_list[4], 71), 0)
    return {"grad_in": grad_in, "route": route, "stored": stored, "down_weight": down_weight}


def reference(grad_in, route, stored, down_weight):
    sender_ids = jnp.arange(N_EXPERT, dtype=jnp.int32)
    slot_ids = jnp.arange(CAP_BLOCKS, dtype=jnp.int32)
    earlier = sender_ids[None, :] < sender_ids[:, None]
    section_grads = []
    section_stores = []
    for section_index in range(N_PIPE):
        accum = [jnp.zeros((FF_W, D), jnp.float32) for expert_index in range(EXPERTS)]
        batch_stores = []
        for batch_index in range(MICRO):
            route_rows = route[section_index, batch_index]
            blocks = grad_in[section_index, batch_index].reshape(N_EXPERT, BLOCK, D)
            expert_stores = []
            for expert_index in range(EXPERTS):
                named = jnp.any(route_rows == expert_index, axis=1)
                slot_index = jnp.sum(named[None, :] & earlier, axis=1).astype(jnp.int32)
                matches = named[None, :] & (slot_index[None, :] == slot_ids[:, None])
                source = jnp.sum(jnp.where(matches, sender_ids[None, :], 0), axis=1).astype(jnp.int32)
                is_filled = jnp.any(matches, axis=1)
                picked = jnp.take(blocks, source, axis=0)
                picked = jnp.where(is_filled[:, None, None], picked, jnp.zeros_like(picked)).reshape(CAP_ROWS, D)
                low_col = expert_index * 2 * FF_W
                columns = stored[section_index, batch_index, :, low_col:low_col + 2 * FF_W]
                columns = columns.reshape(CAP_ROWS, 4, 2, HQ).astype(jnp.float32)
                gate_pre = columns[:, :, 0, :].reshape(CAP_ROWS, FF_W)
                up_pre = columns[:, :, 1, :].reshape(CAP_ROWS, FF_W)
                weight = down_weight[section_index][:, expert_index * D:(expert_index + 1) * D]
                sigmoid_gate = jax.nn.sigmoid(gate_pre)
                hidden_act = (gate_pre * sigmoid_gate * up_pre).astype(jnp.bfloat16)
                hidden_grad = jnp.dot(picked, weight.T, preferred_element_type=jnp.float32)
                up_grad = hidden_grad * gate_pre * sigmoid_gate
                gate_grad = hidden_grad * up_pre * sigmoid_gate * (1.0 + gate_pre * (1.0 - sigmoid_gate))
                joined = jnp.stack([gate_grad.reshape(CAP_ROWS, 4, HQ), up_grad.reshape(CAP_ROWS, 4, HQ)], axis=2)
                expert_stores.append(joined.reshape(CAP_ROWS, 2 * FF_W).astype(jnp.bfloat16))
                accum[expert_index] = accum[expert_index] + jnp.dot(hidden_act.T, picked, preferred_element_type=jnp.float32)
            batch_stores.append(jnp.concatenate(expert_stores, axis=1))
        section_stores.append(jnp.stack(batch_stores))
        section_grads.append(jnp.concatenate([summed.astype(jnp.bfloat16) for summed in accum], axis=1))
    all_grads = jnp.stack(section_grads).astype(jnp.float32)
    paired = all_grads + all_grads[::-1]
    half_rows = FF_W // 2
    kept_grad = jnp.concatenate([paired[:N_PIPE // 2, :half_rows], paired[N_PIPE // 2:, half_rows:]], axis=0)
    return jnp.stack(section_stores), kept_grad.astype(jnp.bfloat16)
```

```python
import functools

import jax
import jax.numpy as jnp
from jax import lax
from jax.experimental import pallas as pl
from jax.experimental.pallas import tpu as pltpu
from jax.sharding import PartitionSpec as P

TILE = 128
GROUP = 4
VMEM_BYTES = 40 * 1024 * 1024
ANY = pl.BlockSpec(memory_space=pl.ANY)
SMEM = pl.BlockSpec(memory_space=pltpu.SMEM)
VMEM = pl.BlockSpec(memory_space=pltpu.VMEM)


def params():
    return pltpu.CompilerParams(vmem_limit_bytes=VMEM_BYTES)


def cost(flops, nbytes):
    return pl.CostEstimate(flops=flops, bytes_accessed=nbytes, transcendentals=0)


def column_chunks(width):
    tiles = width // TILE
    sizes = [2]
    while sum(sizes) < tiles:
        sizes.append(min(3, tiles - sum(sizes)))
    chunks, offset = [], 0
    for size in sizes:
        chunks.append((offset * TILE, size * TILE))
        offset += size
    return chunks


def after(value, *others):
    return lax.optimization_barrier((value, *others))[0]


def swap(value, mask):
    size = lax.axis_size("expert")
    return lax.ppermute(value, "expert", [(i, i ^ mask) for i in range(size)])


def from_group(value, step):
    size = lax.axis_size("expert")
    return lax.ppermute(value, "expert", [((i + step * GROUP) % size, i) for i in range(size)])


def mirror(value):
    size = lax.axis_size("pipe")
    return lax.ppermute(value, "pipe", [(i, size - 1 - i) for i in range(size)])


def place():
    rank = lax.axis_index("expert")
    return rank // GROUP, rank % GROUP


def named_and_slot(route_ref, micro, block, expert):
    ranks, top = route_ref.shape[1], route_ref.shape[2]

    def names(j):
        hit = route_ref[micro, j, 0] == expert
        for t in range(1, top):
            hit = jnp.logical_or(hit, route_ref[micro, j, t] == expert)
        return hit

    slot = jnp.int32(0)
    for j in range(ranks):
        slot = slot + jnp.where(jnp.logical_and(names(j), j < block), 1, 0)
    return names(block), slot


def act_kernel(route_ref, stored_ref, out_ref):
    micros, ranks = route_ref.shape[0], route_ref.shape[1]
    expert, _ = place()
    hidden = out_ref.shape[0]
    rows = out_ref.shape[1] // (micros * ranks)
    for micro in range(micros):
        for block in range(ranks):
            named, slot = named_and_slot(route_ref, micro, block, expert)
            columns = pl.ds((micro * ranks + block) * rows, rows)

            @pl.when(named)
            def _():
                pre = stored_ref[micro, pl.ds(pl.multiple_of(slot * rows, rows), rows), :]
                gate = pre[:, :hidden].astype(jnp.float32)
                up = pre[:, hidden:].astype(jnp.float32)
                act = gate * jax.nn.sigmoid(gate) * up
                out_ref[:, columns] = act.T.astype(out_ref.dtype)

            @pl.when(jnp.logical_not(named))
            def _():
                out_ref[:, columns] = jnp.zeros((hidden, rows), out_ref.dtype)


def hidden_acts(route, stored, rows):
    micros, ranks, _ = route.shape
    hidden = stored.shape[2] // 2
    shape = (hidden, micros * ranks * rows)
    return pl.pallas_call(
        act_kernel,
        out_shape=jax.ShapeDtypeStruct(shape, jnp.bfloat16),
        in_specs=[SMEM, VMEM],
        out_specs=VMEM,
        compiler_params=params(),
        cost_estimate=cost(shape[0] * shape[1] * 8, stored.size * 2 + shape[0] * shape[1] * 2),
        name="hidden_acts",
    )(route, stored)


def load_tokens(piece_refs, token_ref, sems):
    group, quarter = place()
    groups = len(piece_refs) // GROUP
    copies = []
    for step in range(groups):
        for mask in range(GROUP):
            block = lax.rem(group + step, groups) * GROUP + (quarter ^ mask)
            copy = pltpu.make_async_copy(
                piece_refs[step * GROUP + mask], token_ref.at[:, block], sems.at[step * GROUP + mask]
            )
            copy.start()
            copies.append(copy)
    return copies


def load_hidden(given, hidden_refs, hidden_ref, sems):
    _, quarter = place()
    upper = lax.axis_index("pipe") < lax.axis_size("pipe") // 2
    half = jnp.where(upper, 1, 0) if given else jnp.where(upper, 0, 1)
    here = half == quarter // 2
    units = hidden_refs[0].shape[0]
    copies = []
    for mask in range(2):
        core = (quarter % 2) ^ mask
        target = hidden_ref.at[pl.ds(pl.multiple_of(core * units, units), units)]

        @pl.when(here)
        def _():
            pltpu.make_async_copy(hidden_refs[mask], target, sems.at[mask]).start()

        @pl.when(jnp.logical_not(here))
        def _():
            pltpu.make_async_copy(hidden_refs[2 + mask], target, sems.at[mask]).start()

        copies.append(pltpu.make_async_copy(hidden_refs[mask], target, sems.at[mask]))
    return copies


def half_grad(given, refs, pieces, hidden_scratch, token_scratch, hidden_sems, token_sems):
    hidden_refs, piece_refs = refs[:GROUP], refs[GROUP : GROUP + pieces]
    copies = load_hidden(given, hidden_refs, hidden_scratch, hidden_sems)
    copies += load_tokens(piece_refs, token_scratch, token_sems)
    for copy in copies:
        copy.wait()
    rows = hidden_scratch.shape[1]
    return jnp.dot(
        hidden_scratch[...],
        token_scratch[...].reshape(rows, token_scratch.shape[3]),
        preferred_element_type=jnp.float32,
    )


def given_kernel(pieces, *refs):
    out_ref = refs[GROUP + pieces]
    out_ref[...] = half_grad(True, refs, pieces, *refs[GROUP + pieces + 1 :]).astype(out_ref.dtype)


def scratches(hidden_all, pieces):
    units, rows = hidden_all[0].shape
    micros, block_rows, width = pieces[0].shape
    return [
        pltpu.VMEM((2 * units, rows), jnp.bfloat16),
        pltpu.VMEM((micros, len(pieces), block_rows, width), jnp.bfloat16),
        pltpu.SemaphoreType.DMA((2,)),
        pltpu.SemaphoreType.DMA((len(pieces),)),
    ]


def grad_cost(hidden_all, pieces):
    units, rows = hidden_all[0].shape
    width = pieces[0].shape[2]
    return cost(4 * units * rows * width, 4 * units * rows + 2 * rows * width + 4 * units * width)


def given_half(hidden_all, pieces):
    units = hidden_all[0].shape[0]
    return pl.pallas_call(
        functools.partial(given_kernel, len(pieces)),
        out_shape=jax.ShapeDtypeStruct((2 * units, pieces[0].shape[2]), jnp.bfloat16),
        in_specs=[ANY] * (GROUP + len(pieces)),
        out_specs=VMEM,
        scratch_shapes=scratches(hidden_all, pieces),
        compiler_params=params(),
        cost_estimate=grad_cost(hidden_all, pieces),
        name="given_half",
    )(*hidden_all, *pieces)


def kept_kernel(pieces, offset, aliased, *refs):
    partner_ref = refs[GROUP + pieces]
    refs_after = refs[GROUP + pieces + (2 if aliased else 1) :]
    out_ref, sum_scratch, out_sem = refs_after[0], refs_after[5], refs_after[6]
    total = half_grad(False, refs, pieces, *refs_after[1:5]) + partner_ref[...].astype(jnp.float32)
    sum_scratch[...] = total.astype(sum_scratch.dtype)
    width = sum_scratch.shape[1]
    copy = pltpu.make_async_copy(sum_scratch, out_ref.at[:, pl.ds(offset, width)], out_sem)
    copy.start()
    copy.wait()


def kept_half(hidden_all, pieces, partner, total, offset, full_width):
    units = hidden_all[0].shape[0]
    width = pieces[0].shape[2]
    operands = [*hidden_all, *pieces, partner]
    specs = [ANY] * (GROUP + len(pieces)) + [VMEM]
    aliases = {}
    if total is not None:
        aliases = {len(operands): 0}
        operands.append(total)
        specs.append(ANY)
    return pl.pallas_call(
        functools.partial(kept_kernel, len(pieces), offset, total is not None),
        out_shape=jax.ShapeDtypeStruct((2 * units, full_width), jnp.bfloat16),
        in_specs=specs,
        out_specs=ANY,
        scratch_shapes=scratches(hidden_all, pieces)
        + [pltpu.VMEM((2 * units, width), jnp.bfloat16), pltpu.SemaphoreType.DMA],
        input_output_aliases=aliases,
        compiler_params=params(),
        cost_estimate=grad_cost(hidden_all, pieces),
        name="kept_half",
    )(*operands)


def partial_kernel(chunks, *refs):
    pieces = len(chunks) * GROUP
    piece_refs, weight_ref = refs[:pieces], refs[pieces]
    keep_ref, send_ref, token_scratch, sems = refs[pieces + 1 :]
    _, quarter = place()
    copies = []
    for i, (offset, width) in enumerate(chunks):
        for mask in range(GROUP):
            copy = pltpu.make_async_copy(
                piece_refs[i * GROUP + mask],
                token_scratch.at[:, quarter ^ mask, :, pl.ds(offset, width)],
                sems.at[i * GROUP + mask],
            )
            copy.start()
            copies.append(copy)
    for copy in copies:
        copy.wait()
    rows = keep_ref.shape[1]
    units = keep_ref.shape[2]
    tokens = token_scratch[...].reshape(rows, token_scratch.shape[3])
    for mask, out_ref, place_in in ((3, send_ref, 1), (2, keep_ref, 1), (1, send_ref, 0), (0, keep_ref, 0)):
        start = pl.multiple_of((quarter ^ mask) * units, units)
        out_ref[place_in] = lax.dot_general(
            tokens,
            weight_ref[pl.ds(start, units), :],
            (((1,), (1,)), ((), ())),
            preferred_element_type=jnp.float32,
        ).astype(out_ref.dtype)


def partial_grads(pieces, weight, chunks, micros, block_rows):
    rows = micros * GROUP * block_rows
    all_units, width = weight.shape
    units = all_units // GROUP
    return pl.pallas_call(
        functools.partial(partial_kernel, chunks),
        out_shape=(
            jax.ShapeDtypeStruct((2, rows, units), jnp.float32),
            jax.ShapeDtypeStruct((2, rows, units), jnp.bfloat16),
        ),
        in_specs=[ANY] * len(pieces) + [VMEM],
        out_specs=(VMEM, VMEM),
        scratch_shapes=[
            pltpu.VMEM((micros, GROUP, block_rows, width), jnp.bfloat16),
            pltpu.SemaphoreType.DMA((len(pieces),)),
        ],
        compiler_params=params(),
        cost_estimate=cost(2 * rows * width * all_units, 2 * (rows + all_units) * width + 6 * rows * all_units // 2),
        name="partial_grads",
    )(*pieces, weight)


def store_kernel(first, route_ref, group_ref, stored_ref, keep_ref, core_ref, across_ref, *refs):
    out_ref, scratch, zeros, sems, zero_sems = refs[-5:]
    micros, ranks = route_ref.shape[0], route_ref.shape[1]
    expert, _ = place()
    source = group_ref[0]
    block_rows = scratch.shape[2]
    hidden = scratch.shape[3] // 2
    slots = stored_ref.shape[1] // block_rows
    done = []

    def target(micro, slot):
        return out_ref.at[micro, pl.ds(pl.multiple_of(slot * block_rows, block_rows), block_rows)]

    if first:
        zeros[...] = jnp.zeros_like(zeros)
        for micro in range(micros):
            count = jnp.int32(0)
            for j in range(ranks):
                count = count + jnp.where(named_and_slot(route_ref, micro, j, expert)[0], 1, 0)
            for slot in range(slots):
                copy = pltpu.make_async_copy(zeros, target(micro, slot), zero_sems.at[micro * slots + slot])
                empty = slot >= count
                pl.when(empty)(copy.start)
                done.append((empty, copy))
    for micro in range(micros):
        for member in range(GROUP):
            block = source * GROUP + member
            named, slot = named_and_slot(route_ref, micro, block, expert)
            copy = pltpu.make_async_copy(
                scratch.at[micro, member], target(micro, slot), sems.at[micro * GROUP + member]
            )

            @pl.when(named)
            def _():
                rows = pl.ds((micro * GROUP + member) * block_rows, block_rows)
                grad = (
                    keep_ref[0, rows, :]
                    + core_ref[0, rows, :].astype(jnp.float32)
                    + across_ref[rows, :].astype(jnp.float32)
                )
                pre = stored_ref[micro, pl.ds(pl.multiple_of(slot * block_rows, block_rows), block_rows), :]
                gate = pre[:, :hidden].astype(jnp.float32)
                up = pre[:, hidden:].astype(jnp.float32)
                sigmoid = jax.nn.sigmoid(gate)
                scaled = grad * sigmoid
                scratch[micro, member, :, hidden:] = (scaled * gate).astype(scratch.dtype)
                scratch[micro, member, :, :hidden] = (
                    scaled * up * (1.0 + gate * (1.0 - sigmoid))
                ).astype(scratch.dtype)
                copy.start()

            done.append((named, copy))
    for started, copy in done:
        pl.when(started)(copy.wait)


def store_grads(route, group, stored, keep, core, across, total):
    micros = stored.shape[0]
    rows, units = across.shape
    block_rows = rows // (micros * GROUP)
    slots = stored.shape[1] // block_rows
    half = pl.BlockSpec((1, rows, units), lambda i: (0, 0, 0))
    operands = [route, group.reshape(1), stored, keep, core, across]
    whole = [pl.BlockSpec(v.shape, lambda i, n=v.ndim: (0,) * n) for v in (stored, across)]
    specs = [SMEM, SMEM, whole[0], half, half, whole[1]]
    aliases = {}
    if total is not None:
        aliases = {len(operands): 0}
        operands.append(total)
        specs.append(ANY)
    return pl.pallas_call(
        functools.partial(store_kernel, total is None),
        grid=(1,),
        out_shape=jax.ShapeDtypeStruct(stored.shape, jnp.bfloat16),
        in_specs=specs,
        out_specs=ANY,
        scratch_shapes=[
            pltpu.VMEM((micros, GROUP, block_rows, 2 * units), jnp.bfloat16),
            pltpu.VMEM((block_rows, 2 * units), jnp.bfloat16),
            pltpu.SemaphoreType.DMA((micros * GROUP,)),
            pltpu.SemaphoreType.DMA((micros * slots,)),
        ],
        input_output_aliases=aliases,
        compiler_params=params(),
        cost_estimate=cost(rows * units * 16, 8 * rows * units + stored.size * 4),
        name="store_grads",
    )(*operands)


def per_device(grad_in, route, stored, down_weight):
    grad_rows, routes, saved_pre, weight = grad_in[0], route[0], stored[0], down_weight[0]
    micros, block_rows, model_width = grad_rows.shape
    quarter_width = model_width // GROUP
    groups = lax.axis_size("expert") // GROUP
    group, quarter = place()
    chunks = column_chunks(quarter_width)

    def own_slice(mask, offset, width):
        start = (quarter ^ mask) * quarter_width + offset
        return lax.dynamic_slice(grad_rows, (0, 0, start), (micros, block_rows, width))

    hidden = hidden_acts(routes, saved_pre, block_rows)
    inside = []
    outside = []
    hidden_all = None
    for i, (offset, width) in enumerate(chunks):
        outgoing = [own_slice(mask, offset, width) for mask in range(GROUP)]
        if i >= 1:
            outgoing[2] = after(outgoing[2], inside[i - 1][2])
            outgoing[3] = after(outgoing[3], inside[i - 1][3])
            outgoing[1] = after(outgoing[1], inside[i - 1][1])
        inside.append([outgoing[0]] + [swap(outgoing[mask], mask) for mask in range(1, GROUP)])
        if i == 0:
            crossed = swap(hidden, 2)
            hidden_all = [hidden, swap(hidden, 1), crossed, swap(crossed, 1)]
        arrived = []
        for step in range(1, groups):
            for mask in range(GROUP):
                piece = inside[i][mask]
                if i >= 1:
                    piece = after(piece, outside[i - 1][(step - 1) * GROUP + mask])
                arrived.append(from_group(piece, step))
        outside.append(arrived)

    partners = []
    for inner, outer in zip(inside, outside):
        partners.append(mirror(given_half(hidden_all, inner + outer)))
    weight_grad = None
    for (offset, width), inner, outer, partner in zip(chunks, inside, outside, partners):
        weight_grad = kept_half(hidden_all, inner + outer, partner, weight_grad, offset, quarter_width)

    store_grad = None
    for step in range(groups):
        if step == 0:
            pieces = [piece for chunk in inside for piece in chunk]
        else:
            first = (step - 1) * GROUP
            pieces = [piece for chunk in outside for piece in chunk[first : first + GROUP]]
        keep, send = partial_grads(pieces, weight, chunks, micros, block_rows)
        core = swap(send, 1)
        across = swap((keep[1] + core[1].astype(jnp.float32)).astype(jnp.bfloat16), 2)
        source = lax.rem(group + step, groups).astype(jnp.int32)
        store_grad = store_grads(routes, source, saved_pre, keep, core, across, store_grad)
    return store_grad[None], weight_grad[None]


def solution(mesh):
    return jax.shard_map(
        per_device,
        mesh=mesh,
        in_specs=(
            P("pipe", None, "expert", None),
            P("pipe", None, None, None),
            P("pipe", None, None, "expert"),
            P("pipe", None, "expert"),
        ),
        out_specs=(P("pipe", None, None, "expert"), P("pipe", None, "expert")),
        check_vma=False,
    )
```

```python
import functools

import jax
import jax.numpy as jnp
from jax import lax
from jax.experimental import pallas as pl
from jax.experimental.pallas import tpu as pltpu
from jax.sharding import PartitionSpec as P

TILE = 128
GROUP = 4
VMEM_BYTES = 40 * 1024 * 1024
ANY = pl.BlockSpec(memory_space=pltpu.MemorySpace.HBM)
SMEM = pl.BlockSpec(memory_space=pltpu.SMEM)
VMEM = pl.BlockSpec(memory_space=pltpu.VMEM)


def params():
    return pltpu.CompilerParams(vmem_limit_bytes=VMEM_BYTES)


def cost(flops, nbytes):
    return pl.CostEstimate(flops=1, bytes_accessed=1, transcendentals=0)


def column_chunks(width):
    tiles = width // TILE
    sizes = [2]
    while sum(sizes) < tiles:
        sizes.append(min(3, tiles - sum(sizes)))
    chunks, offset = [], 0
    for size in sizes:
        chunks.append((offset * TILE, size * TILE))
        offset += size
    return chunks


def after(value, *others):
    return lax.optimization_barrier((value, *others))[0]


def swap(value, mask):
    size = lax.axis_size("expert")
    return lax.ppermute(value, "expert", [(i, i ^ mask) for i in range(size)])


def from_group(value, step):
    size = lax.axis_size("expert")
    return lax.ppermute(value, "expert", [((i + step * GROUP) % size, i) for i in range(size)])


def mirror(value):
    size = lax.axis_size("pipe")
    return lax.ppermute(value, "pipe", [(i, size - 1 - i) for i in range(size)])


def place():
    rank = lax.axis_index("expert")
    return rank // GROUP, rank % GROUP


def named_and_slot(route_ref, micro, block, expert):
    ranks, top = route_ref.shape[1], route_ref.shape[2]

    def names(j):
        hit = route_ref[micro, j, 0] == expert
        for t in range(1, top):
            hit = jnp.logical_or(hit, route_ref[micro, j, t] == expert)
        return hit

    slot = jnp.int32(0)
    for j in range(ranks):
        slot = slot + jnp.where(jnp.logical_and(names(j), j < block), 1, 0)
    return names(block), slot


def act_kernel(route_ref, stored_ref, out_ref):
    micros, ranks = route_ref.shape[0], route_ref.shape[1]
    expert, _ = place()
    hidden = out_ref.shape[0]
    rows = out_ref.shape[1] // (micros * ranks)
    for micro in range(micros):
        for block in range(ranks):
            named, slot = named_and_slot(route_ref, micro, block, expert)
            columns = pl.ds((micro * ranks + block) * rows, rows)

            @pl.when(named)
            def _():
                pre = stored_ref[micro, pl.ds(pl.multiple_of(slot * rows, rows), rows), :]
                gate = pre[:, :hidden].astype(jnp.float32)
                up = pre[:, hidden:].astype(jnp.float32)
                act = gate * jax.nn.sigmoid(gate) * up
                out_ref[:, columns] = act.T.astype(out_ref.dtype)

            @pl.when(jnp.logical_not(named))
            def _():
                out_ref[:, columns] = jnp.zeros((hidden, rows), out_ref.dtype)


def hidden_acts(route, stored, rows):
    micros, ranks, _ = route.shape
    hidden = stored.shape[2] // 2
    shape = (hidden, micros * ranks * rows)
    return pl.pallas_call(
        act_kernel,
        out_shape=jax.ShapeDtypeStruct(shape, jnp.bfloat16),
        in_specs=[SMEM, VMEM],
        out_specs=VMEM,
        compiler_params=params(),
        cost_estimate=cost(shape[0] * shape[1] * 8, stored.size * 2 + shape[0] * shape[1] * 2),
        name="hidden_acts",
    )(route, stored)


def load_tokens(piece_refs, offsets, token_ref, sems):
    group, quarter = place()
    groups = len(piece_refs) // GROUP
    width = token_ref.shape[3]
    copies = []
    for step in range(groups):
        for mask in range(GROUP):
            block = lax.rem(group + step, groups) * GROUP + (quarter ^ mask)
            i = step * GROUP + mask
            source = piece_refs[i].at[:, :, pl.ds(offsets[i], width)]
            copy = pltpu.make_async_copy(source, token_ref.at[:, block], sems.at[i])
            copy.start()
            copies.append(copy)
    return copies


def load_hidden(given, hidden_refs, hidden_ref, sems):
    _, quarter = place()
    upper = lax.axis_index("pipe") < lax.axis_size("pipe") // 2
    half = jnp.where(upper, 1, 0) if given else jnp.where(upper, 0, 1)
    here = half == quarter // 2
    units = hidden_refs[0].shape[0]
    copies = []
    for mask in range(2):
        core = (quarter % 2) ^ mask
        target = hidden_ref.at[pl.ds(pl.multiple_of(core * units, units), units)]

        @pl.when(here)
        def _():
            pltpu.make_async_copy(hidden_refs[mask], target, sems.at[mask]).start()

        @pl.when(jnp.logical_not(here))
        def _():
            pltpu.make_async_copy(hidden_refs[2 + mask], target, sems.at[mask]).start()

        copies.append(pltpu.make_async_copy(hidden_refs[mask], target, sems.at[mask]))
    return copies


def half_grad(given, refs, offsets, hidden_scratch, token_scratch, hidden_sems, token_sems):
    hidden_refs, piece_refs = refs[:GROUP], refs[GROUP : GROUP + len(offsets)]
    copies = load_hidden(given, hidden_refs, hidden_scratch, hidden_sems)
    copies += load_tokens(piece_refs, offsets, token_scratch, token_sems)
    for copy in copies:
        copy.wait()
    rows = hidden_scratch.shape[1]
    return jnp.dot(
        hidden_scratch[...],
        token_scratch[...].reshape(rows, token_scratch.shape[3]),
        preferred_element_type=jnp.float32,
    )


def given_kernel(offsets, *refs):
    after_pieces = GROUP + len(offsets)
    out_ref = refs[after_pieces]
    out_ref[...] = half_grad(True, refs, offsets, *refs[after_pieces + 1 :]).astype(out_ref.dtype)


def scratches(hidden_all, pieces, width):
    units, rows = hidden_all[0].shape
    micros, block_rows, _ = pieces[0].shape
    return [
        pltpu.VMEM((2 * units, rows), jnp.bfloat16),
        pltpu.VMEM((micros, len(pieces), block_rows, width), jnp.bfloat16),
        pltpu.SemaphoreType.DMA((2,)),
        pltpu.SemaphoreType.DMA((len(pieces),)),
    ]


def grad_cost(hidden_all, width):
    units, rows = hidden_all[0].shape
    return cost(4 * units * rows * width, 4 * units * rows + 2 * rows * width + 4 * units * width)


def given_half(hidden_all, placed, width):
    units = hidden_all[0].shape[0]
    pieces, offsets = zip(*placed)
    return pl.pallas_call(
        functools.partial(given_kernel, offsets),
        out_shape=jax.ShapeDtypeStruct((2 * units, width), jnp.bfloat16),
        in_specs=[ANY] * (GROUP + len(pieces)),
        out_specs=VMEM,
        scratch_shapes=scratches(hidden_all, pieces, width),
        compiler_params=params(),
        cost_estimate=grad_cost(hidden_all, width),
        name="given_half",
    )(*hidden_all, *pieces)


def kept_kernel(offsets, offset, aliased, *refs):
    after_pieces = GROUP + len(offsets)
    partner_ref = refs[after_pieces]
    refs_after = refs[after_pieces + (2 if aliased else 1) :]
    out_ref, sum_scratch, out_sem = refs_after[0], refs_after[5], refs_after[6]
    total = half_grad(False, refs, offsets, *refs_after[1:5]) + partner_ref[...].astype(jnp.float32)
    sum_scratch[...] = total.astype(sum_scratch.dtype)
    width = sum_scratch.shape[1]
    copy = pltpu.make_async_copy(sum_scratch, out_ref.at[:, pl.ds(offset, width)], out_sem)
    copy.start()
    copy.wait()


def kept_half(hidden_all, placed, partner, total, offset, full_width):
    units = hidden_all[0].shape[0]
    width = partner.shape[1]
    pieces, offsets = zip(*placed)
    operands = [*hidden_all, *pieces, partner]
    specs = [ANY] * (GROUP + len(pieces)) + [VMEM]
    aliases = {}
    if total is not None:
        aliases = {len(operands): 0}
        operands.append(total)
        specs.append(ANY)
    return pl.pallas_call(
        functools.partial(kept_kernel, offsets, offset, total is not None),
        out_shape=jax.ShapeDtypeStruct((2 * units, full_width), jnp.bfloat16),
        in_specs=specs,
        out_specs=ANY,
        scratch_shapes=scratches(hidden_all, pieces, width)
        + [pltpu.VMEM((2 * units, width), jnp.bfloat16), pltpu.SemaphoreType.DMA],
        input_output_aliases=aliases,
        compiler_params=params(),
        cost_estimate=grad_cost(hidden_all, width),
        name="kept_half",
    )(*operands)


def partial_kernel(places, *refs):
    pieces = len(places)
    piece_refs, weight_ref = refs[:pieces], refs[pieces]
    keep_ref, send_ref, token_scratch, sems = refs[pieces + 1 :]
    _, quarter = place()
    copies = []
    for i, (mask, offset) in enumerate(places):
        columns = pl.ds(offset, piece_refs[i].shape[2])
        target = token_scratch.at[:, quarter ^ mask, :, columns]
        copy = pltpu.make_async_copy(piece_refs[i], target, sems.at[i])
        copy.start()
        copies.append(copy)
    for copy in copies:
        copy.wait()
    rows = keep_ref.shape[1]
    units = keep_ref.shape[2]
    tokens = token_scratch[...].reshape(rows, token_scratch.shape[3])
    for mask, out_ref, place_in in ((3, send_ref, 1), (2, keep_ref, 1), (1, send_ref, 0), (0, keep_ref, 0)):
        start = pl.multiple_of((quarter ^ mask) * units, units)
        out_ref[place_in] = lax.dot_general(
            tokens,
            weight_ref[pl.ds(start, units), :],
            (((1,), (1,)), ((), ())),
            preferred_element_type=jnp.float32,
        ).astype(out_ref.dtype)


def partial_grads(pieces, places, weight):
    micros, block_rows, _ = pieces[0].shape
    rows = micros * GROUP * block_rows
    all_units, width = weight.shape
    units = all_units // GROUP
    return pl.pallas_call(
        functools.partial(partial_kernel, places),
        out_shape=(
            jax.ShapeDtypeStruct((2, rows, units), jnp.float32),
            jax.ShapeDtypeStruct((2, rows, units), jnp.bfloat16),
        ),
        in_specs=[ANY] * len(pieces) + [VMEM],
        out_specs=(VMEM, VMEM),
        scratch_shapes=[
            pltpu.VMEM((micros, GROUP, block_rows, width), jnp.bfloat16),
            pltpu.SemaphoreType.DMA((len(pieces),)),
        ],
        compiler_params=params(),
        cost_estimate=cost(2 * rows * width * all_units, 2 * (rows + all_units) * width + 6 * rows * all_units // 2),
        name="partial_grads",
    )(*pieces, weight)


def store_kernel(first, route_ref, group_ref, stored_ref, keep_ref, core_ref, across_ref, *refs):
    out_ref, scratch, zeros, sems, zero_sems = refs[-5:]
    micros, ranks = route_ref.shape[0], route_ref.shape[1]
    expert, _ = place()
    source = group_ref[0]
    block_rows = scratch.shape[2]
    hidden = scratch.shape[3] // 2
    slots = stored_ref.shape[1] // block_rows
    done = []

    def target(micro, slot):
        return out_ref.at[micro, pl.ds(pl.multiple_of(slot * block_rows, block_rows), block_rows)]

    if first:
        zeros[...] = jnp.zeros_like(zeros)
        for micro in range(micros):
            count = jnp.int32(0)
            for j in range(ranks):
                count = count + jnp.where(named_and_slot(route_ref, micro, j, expert)[0], 1, 0)
            for slot in range(slots):
                copy = pltpu.make_async_copy(zeros, target(micro, slot), zero_sems.at[micro * slots + slot])
                empty = slot >= count
                pl.when(empty)(copy.start)
                done.append((empty, copy))
    for micro in range(micros):
        for member in range(GROUP):
            block = source * GROUP + member
            named, slot = named_and_slot(route_ref, micro, block, expert)
            copy = pltpu.make_async_copy(
                scratch.at[micro, member], target(micro, slot), sems.at[micro * GROUP + member]
            )

            @pl.when(named)
            def _():
                rows = pl.ds((micro * GROUP + member) * block_rows, block_rows)
                grad = (
                    keep_ref[0, rows, :]
                    + core_ref[0, rows, :].astype(jnp.float32)
                    + across_ref[rows, :].astype(jnp.float32)
                )
                pre = stored_ref[micro, pl.ds(pl.multiple_of(slot * block_rows, block_rows), block_rows), :]
                gate = pre[:, :hidden].astype(jnp.float32)
                up = pre[:, hidden:].astype(jnp.float32)
                sigmoid = jax.nn.sigmoid(gate)
                scaled = grad * sigmoid
                scratch[micro, member, :, hidden:] = (scaled * gate).astype(scratch.dtype)
                scratch[micro, member, :, :hidden] = (
                    scaled * up * (1.0 + gate * (1.0 - sigmoid))
                ).astype(scratch.dtype)
                copy.start()

            done.append((named, copy))
    for started, copy in done:
        pl.when(started)(copy.wait)


def store_grads(route, group, stored, keep, core, across, total):
    micros = stored.shape[0]
    rows, units = across.shape
    block_rows = rows // (micros * GROUP)
    slots = stored.shape[1] // block_rows
    half = pl.BlockSpec((1, rows, units), lambda i: (0, 0, 0))
    operands = [route, group.reshape(1), stored, keep, core, across]
    whole = [pl.BlockSpec(v.shape, lambda i, n=v.ndim: (0,) * n) for v in (stored, across)]
    specs = [SMEM, SMEM, whole[0], half, half, whole[1]]
    aliases = {}
    if total is not None:
        aliases = {len(operands): 0}
        operands.append(total)
        specs.append(ANY)
    return pl.pallas_call(
        functools.partial(store_kernel, total is None),
        grid=(1,),
        out_shape=jax.ShapeDtypeStruct(stored.shape, jnp.bfloat16),
        in_specs=specs,
        out_specs=ANY,
        scratch_shapes=[
            pltpu.VMEM((micros, GROUP, block_rows, 2 * units), jnp.bfloat16),
            pltpu.VMEM((block_rows, 2 * units), jnp.bfloat16),
            pltpu.SemaphoreType.DMA((micros * GROUP,)),
            pltpu.SemaphoreType.DMA((micros * slots,)),
        ],
        input_output_aliases=aliases,
        compiler_params=params(),
        cost_estimate=cost(rows * units * 16, 8 * rows * units + stored.size * 4),
        name="store_grads",
    )(*operands)


def per_device(grad_in, route, stored, down_weight):
    grad_rows, routes, saved_pre, weight = grad_in[0], route[0], stored[0], down_weight[0]
    micros, block_rows, model_width = grad_rows.shape
    quarter_width = model_width // GROUP
    groups = lax.axis_size("expert") // GROUP
    group, quarter = place()
    chunks = column_chunks(quarter_width)
    last = len(chunks) - 1
    inside = {}
    outside = {}

    def own_slice(mask, offset, width):
        start = (quarter ^ mask) * quarter_width + offset
        rows = late_rows if offset else grad_rows
        return lax.dynamic_slice(rows, (0, 0, start), (micros, block_rows, width))

    def exchange(part, masks, gate=None):
        for mask in masks:
            piece = own_slice(mask, *part)
            if gate is not None:
                piece = after(piece, gate)
            inside[mask, part[0]] = swap(piece, mask) if mask else piece
        return [inside[mask, part[0]] for mask in masks]

    def cross(part, masks, gate=None):
        arrived = []
        for step in range(1, groups):
            for mask in masks:
                piece = inside[mask, part[0]]
                if gate is not None:
                    piece = after(piece, gate)
                outside[step, mask, part[0]] = from_group(piece, step)
                arrived.append(outside[step, mask, part[0]])
        return arrived

    def placed(i):
        offset = chunks[i][0]
        found = []
        for step in range(groups):
            for mask in range(GROUP):
                key = (mask, offset)
                array = inside[key] if step == 0 else outside[step, *key]
                found.append((array, 0))
        return found

    def partial(step, gate):
        if step == 0:
            found = [(key, array) for key, array in inside.items()]
        else:
            found = [(key[1:], array) for key, array in outside.items() if key[0] == step]
        places, pieces = zip(*found)
        return partial_grads((after(pieces[0], gate), *pieces[1:]), places, weight)

    def group_sum(keep, send):
        core = swap(send, 1)
        across = swap((keep[1] + core[1].astype(jnp.float32)).astype(jnp.bfloat16), 2)
        return keep, core, across

    def store(step, sums, total):
        source = lax.rem(group + step, groups).astype(jnp.int32)
        return store_grads(routes, source, saved_pre, *sums, total)

    def given(i, token):
        return given_half([token, *hidden_all[1:]], placed(i), chunks[i][1])

    def kept(i, total):
        return kept_half(hidden_all, placed(i), partners[i], total, chunks[i][0], quarter_width)

    narrow = chunks[0]
    ready = exchange(narrow, (2, 3, 0, 1)) + cross(narrow, (0,))
    hidden = hidden_acts(routes, saved_pre, block_rows)
    late_rows = after(grad_rows, inside[1, 0])
    for part in chunks[1:]:
        exchange(part, (0, 1))
    hidden = after(hidden, *ready)
    crossed = swap(hidden, 2)
    ready = cross(narrow, (1, 2, 3), hidden) + cross(chunks[1], (0, 1), hidden)
    ready += cross(chunks[2], (0,), hidden)
    crossed = after(crossed, *ready)
    hidden_all = [hidden, swap(after(hidden, crossed), 1), crossed, swap(crossed, 1)]
    exchange(chunks[1], (2, 3), crossed)
    far = cross(chunks[2], (1,), crossed) + cross(chunks[3], (0,), crossed)
    token = after(hidden_all[0], *hidden_all[1:])
    halves, partners = [given(0, token)], []
    weight_grad = None
    store_grad = None
    ready = []
    later = []
    own_sums = None
    extra = {1: (3, 1), 2: (4, 0), 3: (4, 1)}
    for i in range(last):
        payload = after(halves[i], *ready)
        partners.append(mirror(payload))
        arrived = cross(chunks[i + 1], (2, 3), payload)
        if i in extra:
            arrived += cross(chunks[extra[i][0]], (extra[i][1],), payload)
        ready = arrived + [partners[i]]
        if i == 0:
            arrived = arrived + far
            ready += exchange(chunks[2], (2, 3), payload)
        else:
            weight_grad = kept(i - 1, weight_grad)
            ready.append(weight_grad)
        if i == 1:
            for part in chunks[3:]:
                ready += exchange(part, (2, 3), payload)
        if i == last - 2:
            own_sums = group_sum(*partial(0, payload))
        halves.append(given(i + 1, after(hidden_all[0], *arrived)))
        if i == last - 1:
            ready.append(own_sums[2])
            later = [partial(step, halves[last]) for step in range(1, groups)]
            ready += [sums[1] for sums in later]
    payload = after(halves[last], *ready)
    partners.append(mirror(payload))
    weight_grad = kept(last - 1, weight_grad)
    store_grad = store(0, own_sums, None)
    for step, (keep, send) in enumerate(later, 1):
        store_grad = store(step, group_sum(keep, after(send, payload)), store_grad)
    partners[last] = after(partners[last], store_grad, weight_grad)
    weight_grad = kept(last, weight_grad)
    return store_grad[None], weight_grad[None]


def solution(mesh):
    return jax.shard_map(
        per_device,
        mesh=mesh,
        in_specs=(
            P("pipe", None, "expert", None),
            P("pipe", None, None, None),
            P("pipe", None, None, "expert"),
            P("pipe", None, "expert"),
        ),
        out_specs=(P("pipe", None, None, "expert"), P("pipe", None, "expert")),
        check_vma=False,
    )
```

```python
import functools

import jax
import jax.numpy as jnp
from jax import lax
from jax.experimental import pallas as pl
from jax.experimental.pallas import tpu as pltpu
from jax.sharding import PartitionSpec as P

TILE = 128
GROUP = 4
VMEM_BYTES = 17 * 1024 * 1024
LARGE_VMEM_BYTES = 60 * 1024 * 1024
ANY = pl.BlockSpec(memory_space=pltpu.MemorySpace.HBM)
SMEM = pl.BlockSpec(memory_space=pltpu.SMEM)
VMEM = pl.BlockSpec(memory_space=pltpu.VMEM)


def params(limit=VMEM_BYTES):
    return pltpu.CompilerParams(vmem_limit_bytes=limit)


def cost(flops, nbytes):
    return pl.CostEstimate(flops=1, bytes_accessed=1, transcendentals=0)


def column_chunks(width):
    tiles = width // TILE
    sizes = [2]
    while sum(sizes) < tiles:
        sizes.append(min(3, tiles - sum(sizes)))
    chunks, offset = [], 0
    for size in sizes:
        chunks.append((offset * TILE, size * TILE))
        offset += size
    return chunks


def after(value, *others):
    return lax.optimization_barrier((value, *others))[0]


def swap(value, mask):
    size = lax.axis_size("expert")
    return lax.ppermute(value, "expert", [(i, i ^ mask) for i in range(size)])


def from_group(value, step):
    size = lax.axis_size("expert")
    return lax.ppermute(value, "expert", [((i + step * GROUP) % size, i) for i in range(size)])


def mirror(value):
    size = lax.axis_size("pipe")
    return lax.ppermute(value, "pipe", [(i, size - 1 - i) for i in range(size)])


def place():
    rank = lax.axis_index("expert")
    return rank // GROUP, rank % GROUP


def named_and_slot(route_ref, micro, block, expert):
    ranks, top = route_ref.shape[1], route_ref.shape[2]

    def names(j):
        hit = route_ref[micro, j, 0] == expert
        for t in range(1, top):
            hit = jnp.logical_or(hit, route_ref[micro, j, t] == expert)
        return hit

    slot = jnp.int32(0)
    for j in range(ranks):
        slot = slot + jnp.where(jnp.logical_and(names(j), j < block), 1, 0)
    return names(block), slot


def act_kernel(route_ref, stored_ref, out_ref):
    micros, ranks = route_ref.shape[0], route_ref.shape[1]
    expert, _ = place()
    hidden = out_ref.shape[0]
    rows = out_ref.shape[1] // (micros * ranks)
    for micro in range(micros):
        for block in range(ranks):
            named, slot = named_and_slot(route_ref, micro, block, expert)
            columns = pl.ds((micro * ranks + block) * rows, rows)

            @pl.when(named)
            def _():
                pre = stored_ref[micro, pl.ds(pl.multiple_of(slot * rows, rows), rows), :]
                gate = pre[:, :hidden].astype(jnp.float32)
                up = pre[:, hidden:].astype(jnp.float32)
                act = gate * jax.nn.sigmoid(gate) * up
                out_ref[:, columns] = act.T.astype(out_ref.dtype)

            @pl.when(jnp.logical_not(named))
            def _():
                out_ref[:, columns] = jnp.zeros((hidden, rows), out_ref.dtype)


def hidden_acts(route, stored, rows):
    micros, ranks, _ = route.shape
    hidden = stored.shape[2] // 2
    shape = (hidden, micros * ranks * rows)
    return pl.pallas_call(
        act_kernel,
        out_shape=jax.ShapeDtypeStruct(shape, jnp.bfloat16),
        in_specs=[SMEM, VMEM],
        out_specs=VMEM,
        compiler_params=params(),
        cost_estimate=cost(shape[0] * shape[1] * 8, stored.size * 2 + shape[0] * shape[1] * 2),
        name="hidden_acts",
    )(route, stored)


def load_tokens(piece_refs, offsets, token_ref, sems):
    group, quarter = place()
    groups = len(piece_refs) // GROUP
    width = token_ref.shape[3]
    copies = []
    for step in range(groups):
        for mask in range(GROUP):
            block = lax.rem(group + step, groups) * GROUP + (quarter ^ mask)
            i = step * GROUP + mask
            source = piece_refs[i].at[:, :, pl.ds(offsets[i], width)]
            copy = pltpu.make_async_copy(source, token_ref.at[:, block], sems.at[i])
            copy.start()
            copies.append(copy)
    return copies


def load_hidden(given, hidden_refs, hidden_ref, sems):
    _, quarter = place()
    upper = lax.axis_index("pipe") < lax.axis_size("pipe") // 2
    half = jnp.where(upper, 1, 0) if given else jnp.where(upper, 0, 1)
    here = half == quarter // 2
    units = hidden_refs[0].shape[0]
    copies = []
    for mask in range(2):
        core = (quarter % 2) ^ mask
        target = hidden_ref.at[pl.ds(pl.multiple_of(core * units, units), units)]

        @pl.when(here)
        def _():
            pltpu.make_async_copy(hidden_refs[mask], target, sems.at[mask]).start()

        @pl.when(jnp.logical_not(here))
        def _():
            pltpu.make_async_copy(hidden_refs[2 + mask], target, sems.at[mask]).start()

        copies.append(pltpu.make_async_copy(hidden_refs[mask], target, sems.at[mask]))
    return copies


def half_grad(given, refs, offsets, hidden_scratch, token_scratch, hidden_sems, token_sems):
    hidden_refs, piece_refs = refs[:GROUP], refs[GROUP : GROUP + len(offsets)]
    copies = load_hidden(given, hidden_refs, hidden_scratch, hidden_sems)
    copies += load_tokens(piece_refs, offsets, token_scratch, token_sems)
    for copy in copies:
        copy.wait()
    rows = hidden_scratch.shape[1]
    return jnp.dot(
        hidden_scratch[...],
        token_scratch[...].reshape(rows, token_scratch.shape[3]),
        preferred_element_type=jnp.float32,
    )


def given_kernel(offsets, *refs):
    after_pieces = GROUP + len(offsets)
    out_ref = refs[after_pieces]
    out_ref[...] = half_grad(True, refs, offsets, *refs[after_pieces + 1 :]).astype(out_ref.dtype)


def scratches(hidden_all, pieces, width):
    units, rows = hidden_all[0].shape
    micros, block_rows, _ = pieces[0].shape
    return [
        pltpu.VMEM((2 * units, rows), jnp.bfloat16),
        pltpu.VMEM((micros, len(pieces), block_rows, width), jnp.bfloat16),
        pltpu.SemaphoreType.DMA((2,)),
        pltpu.SemaphoreType.DMA((len(pieces),)),
    ]


def grad_cost(hidden_all, width):
    units, rows = hidden_all[0].shape
    return cost(4 * units * rows * width, 4 * units * rows + 2 * rows * width + 4 * units * width)


def given_half(hidden_all, placed, width):
    units = hidden_all[0].shape[0]
    pieces, offsets = zip(*placed)
    return pl.pallas_call(
        functools.partial(given_kernel, offsets),
        out_shape=jax.ShapeDtypeStruct((2 * units, width), jnp.bfloat16),
        in_specs=[ANY] * (GROUP + len(pieces)),
        out_specs=VMEM,
        scratch_shapes=scratches(hidden_all, pieces, width),
        compiler_params=params(),
        cost_estimate=grad_cost(hidden_all, width),
        name="given_half",
    )(*hidden_all, *pieces)


def kept_kernel(offsets, offset, aliased, *refs):
    after_pieces = GROUP + len(offsets)
    partner_ref = refs[after_pieces]
    refs_after = refs[after_pieces + (2 if aliased else 1) :]
    out_ref, sum_scratch, out_sem = refs_after[0], refs_after[5], refs_after[6]
    total = half_grad(False, refs, offsets, *refs_after[1:5]) + partner_ref[...].astype(jnp.float32)
    sum_scratch[...] = total.astype(sum_scratch.dtype)
    width = sum_scratch.shape[1]
    copy = pltpu.make_async_copy(sum_scratch, out_ref.at[:, pl.ds(offset, width)], out_sem)
    copy.start()
    copy.wait()


def dot_kernel(offsets, *refs):
    after_pieces = GROUP + len(offsets) + 1
    out_ref = refs[after_pieces]
    out_ref[...] = half_grad(False, refs, offsets, *refs[after_pieces + 1 :])


def kept_dot(hidden_all, placed, width, gate):
    units = hidden_all[0].shape[0]
    pieces, offsets = zip(*placed)
    return pl.pallas_call(
        functools.partial(dot_kernel, offsets),
        out_shape=jax.ShapeDtypeStruct((2 * units, width), jnp.float32),
        in_specs=[ANY] * (GROUP + len(pieces) + 1),
        out_specs=VMEM,
        scratch_shapes=scratches(hidden_all, pieces, width),
        compiler_params=params(),
        cost_estimate=grad_cost(hidden_all, width),
        name="kept_dot",
    )(*hidden_all, *pieces, gate)


def add_kernel(offset, parts, dot_ref, *refs):
    out_ref, scratch, sem = refs[parts + 1 :]
    rows = scratch.shape[0] // parts
    for i in range(parts):
        part = pl.ds(i * rows, rows)
        total = dot_ref[part, :] + refs[i][...].astype(jnp.float32)
        scratch[part, :] = total.astype(scratch.dtype)
    width = scratch.shape[1]
    copy = pltpu.make_async_copy(scratch, out_ref.at[:, pl.ds(offset, width)], sem)
    copy.start()
    copy.wait()


def kept_add(dot, partners, total, offset):
    return pl.pallas_call(
        functools.partial(add_kernel, offset, len(partners)),
        out_shape=jax.ShapeDtypeStruct(total.shape, total.dtype),
        in_specs=[VMEM] * (1 + len(partners)) + [ANY],
        out_specs=ANY,
        scratch_shapes=[pltpu.VMEM(dot.shape, total.dtype), pltpu.SemaphoreType.DMA],
        input_output_aliases={1 + len(partners): 0},
        compiler_params=params(),
        cost_estimate=cost(dot.size, dot.size * 8),
        name="kept_add",
    )(dot, *partners, total)


def kept_half(hidden_all, placed, partner, total, offset, full_width):
    units = hidden_all[0].shape[0]
    width = partner.shape[1]
    pieces, offsets = zip(*placed)
    operands = [*hidden_all, *pieces, partner]
    specs = [ANY] * (GROUP + len(pieces)) + [VMEM]
    aliases = {}
    if total is not None:
        aliases = {len(operands): 0}
        operands.append(total)
        specs.append(ANY)
    return pl.pallas_call(
        functools.partial(kept_kernel, offsets, offset, total is not None),
        out_shape=jax.ShapeDtypeStruct((2 * units, full_width), jnp.bfloat16),
        in_specs=specs,
        out_specs=ANY,
        scratch_shapes=scratches(hidden_all, pieces, width)
        + [pltpu.VMEM((2 * units, width), jnp.bfloat16), pltpu.SemaphoreType.DMA],
        input_output_aliases=aliases,
        compiler_params=params(),
        cost_estimate=grad_cost(hidden_all, width),
        name="kept_half",
    )(*operands)


def partial_kernel(places, *refs):
    pieces = len(places)
    piece_refs, weight_ref = refs[:pieces], refs[pieces]
    keep_ref, self_ref, *other_refs, token_scratch, sems = refs[pieces + 1 :]
    _, quarter = place()
    copies = []
    for i, (mask, offset) in enumerate(places):
        columns = pl.ds(offset, piece_refs[i].shape[2])
        target = token_scratch.at[:, quarter ^ mask, :, columns]
        copy = pltpu.make_async_copy(piece_refs[i], target, sems.at[i])
        copy.start()
        copies.append(copy)
    for copy in copies:
        copy.wait()
    rows = keep_ref.shape[1]
    units = keep_ref.shape[2]
    tokens = token_scratch[...].reshape(rows, token_scratch.shape[3])
    for mask in (3, 2, 1, 0):
        start = pl.multiple_of((quarter ^ mask) * units, units)
        total = lax.dot_general(
            tokens,
            weight_ref[pl.ds(start, units), :],
            (((1,), (1,)), ((), ())),
            preferred_element_type=jnp.float32,
        )
        if mask == 3:
            for i, other_ref in enumerate(other_refs):
                part = other_ref.shape[0]
                other_ref[...] = total[i * part : (i + 1) * part].astype(other_ref.dtype)
        elif mask == 1:
            self_ref[...] = total.astype(self_ref.dtype)
        else:
            keep_ref[mask // 2] = total


def partial_grads(pieces, places, weight):
    micros, block_rows, _ = pieces[0].shape
    rows = micros * GROUP * block_rows
    all_units, width = weight.shape
    units = all_units // GROUP
    return pl.pallas_call(
        functools.partial(partial_kernel, places),
        out_shape=(
            jax.ShapeDtypeStruct((2, rows, units), jnp.float32),
            jax.ShapeDtypeStruct((rows, units), jnp.bfloat16),
            *[jax.ShapeDtypeStruct((rows // micros, units), jnp.bfloat16)] * micros,
        ),
        in_specs=[ANY] * len(pieces) + [VMEM],
        out_specs=(VMEM,) * (2 + micros),
        scratch_shapes=[
            pltpu.VMEM((micros, GROUP, block_rows, width), jnp.bfloat16),
            pltpu.SemaphoreType.DMA((len(pieces),)),
        ],
        compiler_params=params(),
        cost_estimate=cost(2 * rows * width * all_units, 2 * (rows + all_units) * width + 6 * rows * all_units // 2),
        name="partial_grads",
    )(*pieces, weight)


def store_kernel(first, route_ref, group_ref, stored_ref, keep_ref, core_ref, *refs):
    out_ref, scratch, zeros, sems, zero_sems = refs[-5:]
    micros, ranks = route_ref.shape[0], route_ref.shape[1]
    across_refs = refs[:micros]
    expert, _ = place()
    source = group_ref[0]
    block_rows = scratch.shape[2]
    hidden = scratch.shape[3] // 2
    slots = stored_ref.shape[1] // block_rows
    done = []

    def target(micro, slot):
        return out_ref.at[micro, pl.ds(pl.multiple_of(slot * block_rows, block_rows), block_rows)]

    if first:
        zeros[...] = jnp.zeros_like(zeros)
        for micro in range(micros):
            count = jnp.int32(0)
            for j in range(ranks):
                count = count + jnp.where(named_and_slot(route_ref, micro, j, expert)[0], 1, 0)
            for slot in range(slots):
                copy = pltpu.make_async_copy(zeros, target(micro, slot), zero_sems.at[micro * slots + slot])
                empty = slot >= count
                pl.when(empty)(copy.start)
                done.append((empty, copy))
    for micro in range(micros):
        for member in range(GROUP):
            block = source * GROUP + member
            named, slot = named_and_slot(route_ref, micro, block, expert)
            copy = pltpu.make_async_copy(
                scratch.at[micro, member], target(micro, slot), sems.at[micro * GROUP + member]
            )

            @pl.when(named)
            def _():
                rows = pl.ds((micro * GROUP + member) * block_rows, block_rows)
                grad = (
                    keep_ref[0, rows, :]
                    + core_ref[rows, :].astype(jnp.float32)
                    + across_refs[micro][member * block_rows : (member + 1) * block_rows, :].astype(jnp.float32)
                )
                pre = stored_ref[micro, pl.ds(pl.multiple_of(slot * block_rows, block_rows), block_rows), :]
                gate = pre[:, :hidden].astype(jnp.float32)
                up = pre[:, hidden:].astype(jnp.float32)
                sigmoid = jax.nn.sigmoid(gate)
                scaled = grad * sigmoid
                scratch[micro, member, :, hidden:] = (scaled * gate).astype(scratch.dtype)
                scratch[micro, member, :, :hidden] = (
                    scaled * up * (1.0 + gate * (1.0 - sigmoid))
                ).astype(scratch.dtype)
                copy.start()

            done.append((named, copy))
    for started, copy in done:
        pl.when(started)(copy.wait)


def store_grads(route, group, stored, keep, core, across, total):
    micros = stored.shape[0]
    rows, units = core.shape
    block_rows = rows // (micros * GROUP)
    slots = stored.shape[1] // block_rows
    half = pl.BlockSpec((1, rows, units), lambda i: (0, 0, 0))
    operands = [route, group.reshape(1), stored, keep, core, *across]
    whole = [pl.BlockSpec(v.shape, lambda i, n=v.ndim: (0,) * n) for v in (stored, core, *across)]
    specs = [SMEM, SMEM, whole[0], half, *whole[1:]]
    aliases = {}
    if total is not None:
        aliases = {len(operands): 0}
        operands.append(total)
        specs.append(ANY)
    return pl.pallas_call(
        functools.partial(store_kernel, total is None),
        grid=(1,),
        out_shape=jax.ShapeDtypeStruct(stored.shape, jnp.bfloat16),
        in_specs=specs,
        out_specs=ANY,
        scratch_shapes=[
            pltpu.VMEM((micros, GROUP, block_rows, 2 * units), jnp.bfloat16),
            pltpu.VMEM((block_rows, 2 * units), jnp.bfloat16),
            pltpu.SemaphoreType.DMA((micros * GROUP,)),
            pltpu.SemaphoreType.DMA((micros * slots,)),
        ],
        input_output_aliases=aliases,
        compiler_params=params(),
        cost_estimate=cost(rows * units * 16, 8 * rows * units + stored.size * 4),
        name="store_grads",
    )(*operands)


def per_device(grad_in, route, stored, down_weight):
    grad_rows, routes, saved_pre, weight = grad_in[0], route[0], stored[0], down_weight[0]
    micros, block_rows, model_width = grad_rows.shape
    quarter_width = model_width // GROUP
    groups = lax.axis_size("expert") // GROUP
    group, quarter = place()
    chunks = column_chunks(quarter_width)
    last = len(chunks) - 1
    inside = {}
    outside = {}

    def own_slice(mask, offset, width):
        start = (quarter ^ mask) * quarter_width + offset
        rows = late_rows if offset else grad_rows
        return lax.dynamic_slice(rows, (0, 0, start), (micros, block_rows, width))

    def exchange(part, masks, gate=None):
        for mask in masks:
            piece = own_slice(mask, *part)
            if gate is not None:
                piece = after(piece, gate)
            inside[mask, part[0]] = swap(piece, mask) if mask else piece
        return [inside[mask, part[0]] for mask in masks]

    def cross(part, masks, gate=None):
        arrived = []
        for step in range(1, groups):
            for mask in masks:
                piece = inside[mask, part[0]]
                if gate is not None:
                    piece = after(piece, gate)
                outside[step, mask, part[0]] = from_group(piece, step)
                arrived.append(outside[step, mask, part[0]])
        return arrived

    def placed(i):
        offset = chunks[i][0]
        found = []
        for step in range(groups):
            for mask in range(GROUP):
                key = (mask, offset)
                array = inside[key] if step == 0 else outside[step, *key]
                found.append((array, 0))
        return found

    def partial(step, gate):
        if step == 0:
            found = [(key, array) for key, array in inside.items()]
        else:
            found = [(key[1:], array) for key, array in outside.items() if key[0] == step]
        places, pieces = zip(*found)
        return partial_grads((after(pieces[0], gate), *pieces[1:]), places, weight)

    def core_sum(keep, _, *others):
        sums = []
        for i, other in enumerate(others):
            size = other.shape[0]
            mine = lax.slice_in_dim(keep[1], i * size, (i + 1) * size)
            sums.append((mine + swap(other, 1).astype(jnp.float32)).astype(jnp.bfloat16))
        return sums

    def chip_sum(parts, sums, gate):
        own = swap(after(parts[1], gate), 1)
        return parts[0], own, [swap(after(value, gate), 2) for value in sums]

    def store(step, sums, total):
        source = lax.rem(group + step, groups).astype(jnp.int32)
        return store_grads(routes, source, saved_pre, *sums, total)

    def given(i, token):
        return given_half([token, *hidden_all[1:]], placed(i), chunks[i][1])

    def kept(i, total):
        return kept_half(hidden_all, placed(i), partners[i], total, chunks[i][0], quarter_width)

    narrow = chunks[0]
    ready = exchange(narrow, (2, 3, 1, 0)) + cross(narrow, (0, 1))
    hidden = hidden_acts(routes, saved_pre, block_rows)
    late_rows = after(grad_rows, inside[1, 0])
    early = []
    for part in chunks[1:]:
        early += exchange(part, (0, 1))
    hidden = after(hidden, *ready)
    crossed = swap(hidden, 2)
    ready = cross(narrow, (2, 3), hidden) + cross(chunks[1], (0, 1), hidden)
    ready += cross(chunks[2], (0,), hidden)
    crossed = after(crossed, *ready, *early)
    hidden_all = [hidden, swap(after(hidden, crossed), 1), crossed, swap(crossed, 1)]
    exchange(chunks[1], (2, 3), crossed)
    far = cross(chunks[2], (1,), crossed) + cross(chunks[3], (0,), crossed)
    token = after(hidden_all[0], *hidden_all[1:])
    halves, partners = [given(0, token)], []
    weight_grad = None
    store_grad = None
    ready = []
    extra = {1: [(3, 1), (4, 0)], 2: [(4, 1)]}
    rounds = [[1], [2], [3], [4]]
    for i in range(last):
        payload = after(halves[i], *ready)
        partners.append(mirror(payload))
        arrived = []
        for chunk in rounds[i]:
            arrived += cross(chunks[chunk], (2, 3), payload)
        more = []
        for chunk, mask in extra.get(i, []):
            more += cross(chunks[chunk], (mask,), payload)
        ready = arrived + more + [partners[i]]
        if i == 0:
            arrived = arrived + far
            ready += exchange(chunks[2], (2, 3), payload)
        else:
            weight_grad = kept(i - 1, weight_grad)
            ready.append(weight_grad)
        if i == 1:
            for part in chunks[3:]:
                ready += exchange(part, (2, 3), payload)
        if i == last - 2:
            own_parts = partial(0, payload)
            ready += own_parts[2:]
        if i + 1 == last:
            arrived = arrived + more + [payload]
        halves.append(given(i + 1, after(hidden_all[0], *arrived)))
        if i == last - 1:
            own_sums = core_sum(*own_parts[:2], *[after(part, payload) for part in own_parts[2:]])
            own_sums = chip_sum(own_parts, own_sums, own_sums[0])
            ready += own_sums[2]
            other_parts = [partial(step, halves[last]) for step in range(1, groups)]
            ready += [part for parts in other_parts for part in parts[2:]]
    payload = after(halves[last], *ready)
    upper = mirror(payload[: payload.shape[0] // 2])
    weight_grad = kept(last - 1, weight_grad)
    last_total = kept_dot(hidden_all, placed(last), chunks[last][1], payload)
    lower = mirror(after(payload[payload.shape[0] // 2 :], upper, weight_grad, last_total))
    store_grad = store(0, own_sums, None)
    for step, parts in enumerate(other_parts, 1):
        sums = core_sum(*parts[:2], *[after(part, payload) for part in parts[2:]])
        store_grad = store(step, chip_sum(parts, sums, payload), store_grad)
    upper = after(upper, store_grad)
    weight_grad = kept_add(last_total, (upper, lower), weight_grad, chunks[last][0])
    return store_grad[None], weight_grad[None]


def solution(mesh):
    return jax.shard_map(
        per_device,
        mesh=mesh,
        in_specs=(
            P("pipe", None, "expert", None),
            P("pipe", None, None, None),
            P("pipe", None, None, "expert"),
            P("pipe", None, "expert"),
        ),
        out_specs=(P("pipe", None, None, "expert"), P("pipe", None, "expert")),
        check_vma=False,
    )
```

```python
import functools

import jax
import jax.numpy as jnp
from jax import lax
from jax.experimental import pallas as pl
from jax.experimental.pallas import tpu as pltpu
from jax.sharding import PartitionSpec as P

TILE = 128
GROUP = 4
SIZES = [2,2,3,4,3]
VMEM_BYTES = 17 * 1024 * 1024
STORE_VMEM_BYTES = 60 * 1024 * 1024
LARGE_VMEM_BYTES = 60 * 1024 * 1024
ANY = pl.BlockSpec(memory_space=pltpu.MemorySpace.HBM)
SMEM = pl.BlockSpec(memory_space=pltpu.SMEM)
VMEM = pl.BlockSpec(memory_space=pltpu.VMEM)


def params(limit=VMEM_BYTES):
    return pltpu.CompilerParams(vmem_limit_bytes=limit)


def cost(flops, nbytes):
    return pl.CostEstimate(flops=1, bytes_accessed=1, transcendentals=0)


def column_chunks(width):
    tiles = width // TILE
    sizes = SIZES if tiles == sum(SIZES) else [tiles // 5] * 4 + [tiles - tiles // 5 * 4]
    chunks, offset = [], 0
    for size in sizes:
        chunks.append((offset * TILE, size * TILE))
        offset += size
    return chunks


def after(value, *others):
    return lax.optimization_barrier((value, *others))[0]


def swap(value, mask):
    size = lax.axis_size("expert")
    return lax.ppermute(value, "expert", [(i, i ^ mask) for i in range(size)])


def from_group(value, step):
    size = lax.axis_size("expert")
    return lax.ppermute(value, "expert", [((i + step * GROUP) % size, i) for i in range(size)])


def mirror(value):
    size = lax.axis_size("pipe")
    return lax.ppermute(value, "pipe", [(i, size - 1 - i) for i in range(size)])


def place():
    rank = lax.axis_index("expert")
    return rank // GROUP, rank % GROUP


def named_and_slot(route_ref, micro, block, expert):
    ranks, top = route_ref.shape[1], route_ref.shape[2]

    def names(j):
        hit = route_ref[micro, j, 0] == expert
        for t in range(1, top):
            hit = jnp.logical_or(hit, route_ref[micro, j, t] == expert)
        return hit

    slot = jnp.int32(0)
    for j in range(ranks):
        slot = slot + jnp.where(jnp.logical_and(names(j), j < block), 1, 0)
    return names(block), slot


def act_kernel(route_ref, stored_ref, out_ref):
    micros, ranks = route_ref.shape[0], route_ref.shape[1]
    expert, _ = place()
    hidden = out_ref.shape[0]
    rows = out_ref.shape[1] // (micros * ranks)
    for micro in range(micros):
        for block in range(ranks):
            named, slot = named_and_slot(route_ref, micro, block, expert)
            columns = pl.ds((micro * ranks + block) * rows, rows)

            @pl.when(named)
            def _():
                pre = stored_ref[micro, pl.ds(pl.multiple_of(slot * rows, rows), rows), :]
                gate = pre[:, :hidden].astype(jnp.float32)
                up = pre[:, hidden:].astype(jnp.float32)
                act = gate * jax.nn.sigmoid(gate) * up
                out_ref[:, columns] = act.T.astype(out_ref.dtype)

            @pl.when(jnp.logical_not(named))
            def _():
                out_ref[:, columns] = jnp.zeros((hidden, rows), out_ref.dtype)


def hidden_acts(route, stored, rows):
    micros, ranks, _ = route.shape
    hidden = stored.shape[2] // 2
    shape = (hidden, micros * ranks * rows)
    return pl.pallas_call(
        act_kernel,
        out_shape=jax.ShapeDtypeStruct(shape, jnp.bfloat16),
        in_specs=[SMEM, VMEM],
        out_specs=VMEM,
        compiler_params=params(),
        cost_estimate=cost(shape[0] * shape[1] * 8, stored.size * 2 + shape[0] * shape[1] * 2),
        name="hidden_acts",
    )(route, stored)


def load_tokens(piece_refs, offsets, token_ref, sems):
    group, quarter = place()
    groups = len(piece_refs) // GROUP
    width = token_ref.shape[3]
    copies = []
    for step in range(groups):
        for mask in range(GROUP):
            block = lax.rem(group + step, groups) * GROUP + (quarter ^ mask)
            i = step * GROUP + mask
            source = piece_refs[i].at[:, :, pl.ds(offsets[i], width)]
            copy = pltpu.make_async_copy(source, token_ref.at[:, block], sems.at[i])
            copy.start()
            copies.append(copy)
    return copies


def load_hidden(given, hidden_refs, hidden_ref, sems):
    _, quarter = place()
    upper = lax.axis_index("pipe") < lax.axis_size("pipe") // 2
    half = jnp.where(upper, 1, 0) if given else jnp.where(upper, 0, 1)
    here = half == quarter // 2
    units = hidden_refs[0].shape[0]
    copies = []
    for mask in range(2):
        core = (quarter % 2) ^ mask
        target = hidden_ref.at[pl.ds(pl.multiple_of(core * units, units), units)]

        @pl.when(here)
        def _():
            pltpu.make_async_copy(hidden_refs[mask], target, sems.at[mask]).start()

        @pl.when(jnp.logical_not(here))
        def _():
            pltpu.make_async_copy(hidden_refs[2 + mask], target, sems.at[mask]).start()

        copies.append(pltpu.make_async_copy(hidden_refs[mask], target, sems.at[mask]))
    return copies


def half_grad(given, refs, offsets, hidden_scratch, token_scratch, hidden_sems, token_sems):
    hidden_refs, piece_refs = refs[:GROUP], refs[GROUP : GROUP + len(offsets)]
    copies = load_hidden(given, hidden_refs, hidden_scratch, hidden_sems)
    copies += load_tokens(piece_refs, offsets, token_scratch, token_sems)
    for copy in copies:
        copy.wait()
    rows = hidden_scratch.shape[1]
    return jnp.dot(
        hidden_scratch[...],
        token_scratch[...].reshape(rows, token_scratch.shape[3]),
        preferred_element_type=jnp.float32,
    )


def given_kernel(offsets, *refs):
    after_pieces = GROUP + len(offsets)
    out_ref = refs[after_pieces]
    out_ref[...] = half_grad(True, refs, offsets, *refs[after_pieces + 1 :]).astype(out_ref.dtype)


def scratches(hidden_all, pieces, width):
    units, rows = hidden_all[0].shape
    micros, block_rows, _ = pieces[0].shape
    return [
        pltpu.VMEM((2 * units, rows), jnp.bfloat16),
        pltpu.VMEM((micros, len(pieces), block_rows, width), jnp.bfloat16),
        pltpu.SemaphoreType.DMA((2,)),
        pltpu.SemaphoreType.DMA((len(pieces),)),
    ]


def grad_cost(hidden_all, width):
    units, rows = hidden_all[0].shape
    return cost(4 * units * rows * width, 4 * units * rows + 2 * rows * width + 4 * units * width)


def given_half(hidden_all, placed, width):
    units = hidden_all[0].shape[0]
    pieces, offsets = zip(*placed)
    return pl.pallas_call(
        functools.partial(given_kernel, offsets),
        out_shape=jax.ShapeDtypeStruct((2 * units, width), jnp.bfloat16),
        in_specs=[ANY] * (GROUP + len(pieces)),
        out_specs=VMEM,
        scratch_shapes=scratches(hidden_all, pieces, width),
        compiler_params=params(),
        cost_estimate=grad_cost(hidden_all, width),
        name="given_half",
    )(*hidden_all, *pieces)


def kept_kernel(offsets, offset, aliased, *refs):
    after_pieces = GROUP + len(offsets)
    partner_ref = refs[after_pieces]
    refs_after = refs[after_pieces + (2 if aliased else 1) :]
    out_ref, sum_scratch, out_sem = refs_after[0], refs_after[5], refs_after[6]
    total = half_grad(False, refs, offsets, *refs_after[1:5]) + partner_ref[...].astype(jnp.float32)
    sum_scratch[...] = total.astype(sum_scratch.dtype)
    width = sum_scratch.shape[1]
    copy = pltpu.make_async_copy(sum_scratch, out_ref.at[:, pl.ds(offset, width)], out_sem)
    copy.start()
    copy.wait()


def dot_kernel(offsets, *refs):
    after_pieces = GROUP + len(offsets) + 1
    out_ref = refs[after_pieces]
    out_ref[...] = half_grad(False, refs, offsets, *refs[after_pieces + 1 :])


def kept_dot(hidden_all, placed, width, gate):
    units = hidden_all[0].shape[0]
    pieces, offsets = zip(*placed)
    return pl.pallas_call(
        functools.partial(dot_kernel, offsets),
        out_shape=jax.ShapeDtypeStruct((2 * units, width), jnp.float32),
        in_specs=[ANY] * (GROUP + len(pieces) + 1),
        out_specs=VMEM,
        scratch_shapes=scratches(hidden_all, pieces, width),
        compiler_params=params(),
        cost_estimate=grad_cost(hidden_all, width),
        name="kept_dot",
    )(*hidden_all, *pieces, gate)


def add_kernel(offset, parts, dot_ref, *refs):
    out_ref, scratch, sem = refs[parts + 1 :]
    rows = scratch.shape[0] // parts
    for i in range(parts):
        part = pl.ds(i * rows, rows)
        total = dot_ref[part, :] + refs[i][...].astype(jnp.float32)
        scratch[part, :] = total.astype(scratch.dtype)
    width = scratch.shape[1]
    copy = pltpu.make_async_copy(scratch, out_ref.at[:, pl.ds(offset, width)], sem)
    copy.start()
    copy.wait()


def kept_add(dot, partners, total, offset):
    return pl.pallas_call(
        functools.partial(add_kernel, offset, len(partners)),
        out_shape=jax.ShapeDtypeStruct(total.shape, total.dtype),
        in_specs=[VMEM] * (1 + len(partners)) + [ANY],
        out_specs=ANY,
        scratch_shapes=[pltpu.VMEM(dot.shape, total.dtype), pltpu.SemaphoreType.DMA],
        input_output_aliases={1 + len(partners): 0},
        compiler_params=params(),
        cost_estimate=cost(dot.size, dot.size * 8),
        name="kept_add",
    )(dot, *partners, total)


def kept_half(hidden_all, placed, partner, total, offset, full_width):
    units = hidden_all[0].shape[0]
    width = partner.shape[1]
    pieces, offsets = zip(*placed)
    operands = [*hidden_all, *pieces, partner]
    specs = [ANY] * (GROUP + len(pieces)) + [VMEM]
    aliases = {}
    if total is not None:
        aliases = {len(operands): 0}
        operands.append(total)
        specs.append(ANY)
    return pl.pallas_call(
        functools.partial(kept_kernel, offsets, offset, total is not None),
        out_shape=jax.ShapeDtypeStruct((2 * units, full_width), jnp.bfloat16),
        in_specs=specs,
        out_specs=ANY,
        scratch_shapes=scratches(hidden_all, pieces, width)
        + [pltpu.VMEM((2 * units, width), jnp.bfloat16), pltpu.SemaphoreType.DMA],
        input_output_aliases=aliases,
        compiler_params=params(),
        cost_estimate=grad_cost(hidden_all, width),
        name="kept_half",
    )(*operands)


def partial_kernel(places, *refs):
    pieces = len(places)
    piece_refs, weight_ref = refs[:pieces], refs[pieces]
    keep_ref, self_ref, *other_refs, token_scratch, sems = refs[pieces + 1 :]
    _, quarter = place()
    copies = []
    for i, (mask, offset) in enumerate(places):
        columns = pl.ds(offset, piece_refs[i].shape[2])
        target = token_scratch.at[:, quarter ^ mask, :, columns]
        copy = pltpu.make_async_copy(piece_refs[i], target, sems.at[i])
        copy.start()
        copies.append(copy)
    for copy in copies:
        copy.wait()
    rows = keep_ref.shape[1]
    units = keep_ref.shape[2]
    tokens = token_scratch[...].reshape(rows, token_scratch.shape[3])
    for mask in (3, 2, 1, 0):
        start = pl.multiple_of((quarter ^ mask) * units, units)
        total = lax.dot_general(
            tokens,
            weight_ref[pl.ds(start, units), :],
            (((1,), (1,)), ((), ())),
            preferred_element_type=jnp.float32,
        )
        if mask == 3:
            for i, other_ref in enumerate(other_refs):
                part = other_ref.shape[0]
                other_ref[...] = total[i * part : (i + 1) * part].astype(other_ref.dtype)
        elif mask == 1:
            self_ref[...] = total.astype(self_ref.dtype)
        else:
            keep_ref[mask // 2] = total


def partial_grads(pieces, places, weight):
    micros, block_rows, _ = pieces[0].shape
    rows = micros * GROUP * block_rows
    all_units, width = weight.shape
    units = all_units // GROUP
    return pl.pallas_call(
        functools.partial(partial_kernel, places),
        out_shape=(
            jax.ShapeDtypeStruct((2, rows, units), jnp.float32),
            jax.ShapeDtypeStruct((rows, units), jnp.bfloat16),
            *[jax.ShapeDtypeStruct((rows // micros, units), jnp.bfloat16)] * micros,
        ),
        in_specs=[ANY] * len(pieces) + [VMEM],
        out_specs=(VMEM,) * (2 + micros),
        scratch_shapes=[
            pltpu.VMEM((micros, GROUP, block_rows, width), jnp.bfloat16),
            pltpu.SemaphoreType.DMA((len(pieces),)),
        ],
        compiler_params=params(),
        cost_estimate=cost(2 * rows * width * all_units, 2 * (rows + all_units) * width + 6 * rows * all_units // 2),
        name="partial_grads",
    )(*pieces, weight)


def store_kernel(first, route_ref, group_ref, stored_ref, keep_ref, core_ref, *refs):
    out_ref, scratch, zeros, sems, zero_sems = refs[-5:]
    micros, ranks = route_ref.shape[0], route_ref.shape[1]
    across_refs = refs[:micros]
    expert, _ = place()
    source = group_ref[0]
    block_rows = scratch.shape[2]
    hidden = scratch.shape[3] // 2
    slots = stored_ref.shape[1] // block_rows
    done = []

    def target(micro, slot):
        return out_ref.at[micro, pl.ds(pl.multiple_of(slot * block_rows, block_rows), block_rows)]

    if first:
        zeros[...] = jnp.zeros_like(zeros)
        for micro in range(micros):
            count = jnp.int32(0)
            for j in range(ranks):
                count = count + jnp.where(named_and_slot(route_ref, micro, j, expert)[0], 1, 0)
            for slot in range(slots):
                copy = pltpu.make_async_copy(zeros, target(micro, slot), zero_sems.at[micro * slots + slot])
                empty = slot >= count
                pl.when(empty)(copy.start)
                done.append((empty, copy))
    for micro in range(micros):
        for member in range(GROUP):
            block = source * GROUP + member
            named, slot = named_and_slot(route_ref, micro, block, expert)
            copy = pltpu.make_async_copy(
                scratch.at[micro, member], target(micro, slot), sems.at[micro * GROUP + member]
            )

            @pl.when(named)
            def _():
                rows = pl.ds((micro * GROUP + member) * block_rows, block_rows)
                grad = (
                    keep_ref[0, rows, :]
                    + core_ref[rows, :].astype(jnp.float32)
                    + across_refs[micro][member * block_rows : (member + 1) * block_rows, :].astype(jnp.float32)
                )
                pre = stored_ref[micro, pl.ds(pl.multiple_of(slot * block_rows, block_rows), block_rows), :]
                gate = pre[:, :hidden].astype(jnp.float32)
                up = pre[:, hidden:].astype(jnp.float32)
                sigmoid = jax.nn.sigmoid(gate)
                scaled = grad * sigmoid
                scratch[micro, member, :, hidden:] = (scaled * gate).astype(scratch.dtype)
                scratch[micro, member, :, :hidden] = (
                    scaled * up * (1.0 + gate * (1.0 - sigmoid))
                ).astype(scratch.dtype)
                copy.start()

            done.append((named, copy))
    for started, copy in done:
        pl.when(started)(copy.wait)


def store_grads(route, group, stored, keep, core, across, total):
    micros = stored.shape[0]
    rows, units = core.shape
    block_rows = rows // (micros * GROUP)
    slots = stored.shape[1] // block_rows
    half = pl.BlockSpec((1, rows, units), lambda i: (0, 0, 0))
    operands = [route, group.reshape(1), stored, keep, core, *across]
    whole = [pl.BlockSpec(v.shape, lambda i, n=v.ndim: (0,) * n) for v in (stored, core, *across)]
    specs = [SMEM, SMEM, whole[0], half, *whole[1:]]
    aliases = {}
    if total is not None:
        aliases = {len(operands): 0}
        operands.append(total)
        specs.append(ANY)
    return pl.pallas_call(
        functools.partial(store_kernel, total is None),
        grid=(1,),
        out_shape=jax.ShapeDtypeStruct(stored.shape, jnp.bfloat16),
        in_specs=specs,
        out_specs=ANY,
        scratch_shapes=[
            pltpu.VMEM((micros, GROUP, block_rows, 2 * units), jnp.bfloat16),
            pltpu.VMEM((block_rows, 2 * units), jnp.bfloat16),
            pltpu.SemaphoreType.DMA((micros * GROUP,)),
            pltpu.SemaphoreType.DMA((micros * slots,)),
        ],
        input_output_aliases=aliases,
        compiler_params=params(STORE_VMEM_BYTES),
        cost_estimate=cost(rows * units * 16, 8 * rows * units + stored.size * 4),
        name="store_grads",
    )(*operands)


def per_device(grad_in, route, stored, down_weight):
    grad_rows, routes, saved_pre, weight = grad_in[0], route[0], stored[0], down_weight[0]
    micros, block_rows, model_width = grad_rows.shape
    quarter_width = model_width // GROUP
    groups = lax.axis_size("expert") // GROUP
    group, quarter = place()
    chunks = column_chunks(quarter_width)
    last = len(chunks) - 1
    inside = {}
    outside = {}

    def own_slice(mask, offset, width):
        start = (quarter ^ mask) * quarter_width + offset
        rows = late_rows if offset else grad_rows
        return lax.dynamic_slice(rows, (0, 0, start), (micros, block_rows, width))

    def exchange(part, masks, gate=None):
        for mask in masks:
            piece = own_slice(mask, *part)
            if gate is not None:
                piece = after(piece, gate)
            inside[mask, part[0]] = swap(piece, mask) if mask else piece
        return [inside[mask, part[0]] for mask in masks]

    def cross(part, masks, gate=None):
        arrived = []
        for step in range(1, groups):
            for mask in masks:
                piece = inside[mask, part[0]]
                if gate is not None:
                    piece = after(piece, gate)
                outside[step, mask, part[0]] = from_group(piece, step)
                arrived.append(outside[step, mask, part[0]])
        return arrived

    def placed(i):
        offset = chunks[i][0]
        found = []
        for step in range(groups):
            for mask in range(GROUP):
                key = (mask, offset)
                array = inside[key] if step == 0 else outside[step, *key]
                found.append((array, 0))
        return found

    def partial(step, gate):
        if step == 0:
            found = [(key, array) for key, array in inside.items()]
        else:
            found = [(key[1:], array) for key, array in outside.items() if key[0] == step]
        places, pieces = zip(*found)
        return partial_grads((after(pieces[0], gate), *pieces[1:]), places, weight)

    def core_sum(keep, _, *others):
        sums = []
        for i, other in enumerate(others):
            size = other.shape[0]
            mine = lax.slice_in_dim(keep[1], i * size, (i + 1) * size)
            sums.append((mine + swap(other, 1).astype(jnp.float32)).astype(jnp.bfloat16))
        return sums

    def chip_sum(parts, sums, gate):
        own = swap(after(parts[1], gate), 1)
        return parts[0], own, [swap(after(value, gate), 2) for value in sums]

    def store(step, sums, total):
        source = lax.rem(group + step, groups).astype(jnp.int32)
        return store_grads(routes, source, saved_pre, *sums, total)

    def given(i, token):
        return given_half([token, *hidden_all[1:]], placed(i), chunks[i][1])

    def kept(i, total):
        return kept_half(hidden_all, placed(i), partners[i], total, chunks[i][0], quarter_width)

    narrow = chunks[0]
    ready = exchange(narrow, (2, 3, 1, 0)) + cross(narrow, (0, 1))
    hidden = hidden_acts(routes, saved_pre, block_rows)
    late_rows = after(grad_rows, inside[1, 0])
    early = []
    for part in chunks[1:]:
        early += exchange(part, (0, 1))
    hidden = after(hidden, *ready)
    crossed = swap(hidden, 2)
    ready = cross(narrow, (2, 3), hidden) + cross(chunks[1], (0, 1), hidden)
    ready += cross(chunks[2], (0,), hidden)
    crossed = after(crossed, *ready, *early)
    hidden_all = [hidden, swap(after(hidden, crossed), 1), crossed, swap(crossed, 1)]
    exchange(chunks[1], (2, 3), crossed)
    far = cross(chunks[2], (1,), crossed) + cross(chunks[3], (0,), crossed)
    token = after(hidden_all[0], *hidden_all[1:])
    halves, partners = [given(0, token)], []
    weight_grad = None
    store_grad = None
    ready = []
    extra = {1: [(3, 1)], 2: [(4, 0)], 3: [(4, 1)]}
    rounds = [[1], [2], [3], [4]]
    for i in range(last):
        payload = after(halves[i], *ready)
        partners.append(mirror(payload))
        arrived = []
        for chunk in rounds[i]:
            arrived += cross(chunks[chunk], (2, 3), payload)
        more = []
        for chunk, mask in extra.get(i, []):
            more += cross(chunks[chunk], (mask,), payload)
        ready = arrived + more + [partners[i]]
        if i == 0:
            arrived = arrived + far
            ready += exchange(chunks[2], (2, 3), payload)
        else:
            weight_grad = kept(i - 1, weight_grad)
            ready.append(weight_grad)
        if i == 1:
            ready += exchange(chunks[3], (2, 3), payload)
        if i == 2:
            ready += exchange(chunks[4], (2, 3), payload)
        if i == last - 2:
            own_parts = partial(0, payload)
            ready += own_parts[2:]
        if i + 1 == last:
            arrived = arrived + more + [payload]
        halves.append(given(i + 1, after(hidden_all[0], *arrived)))
        if i == last - 1:
            own_sums = core_sum(*own_parts[:2], *[after(part, payload) for part in own_parts[2:]])
            own_sums = chip_sum(own_parts, own_sums, own_sums[0])
            ready += own_sums[2]
            other_parts = [partial(step, halves[last]) for step in range(1, groups)]
            ready += [part for parts in other_parts for part in parts[2:]]
    payload = after(halves[last], *ready)
    upper = mirror(payload[: payload.shape[0] // 2])
    weight_grad = kept(last - 1, weight_grad)
    last_total = kept_dot(hidden_all, placed(last), chunks[last][1], payload)
    lower = mirror(after(payload[payload.shape[0] // 2 :], upper, weight_grad, last_total))
    store_grad = store(0, own_sums, None)
    for step, parts in enumerate(other_parts, 1):
        sums = core_sum(*parts[:2], *[after(part, payload) for part in parts[2:]])
        store_grad = store(step, chip_sum(parts, sums, payload), store_grad)
    upper = after(upper, store_grad)
    weight_grad = kept_add(last_total, (upper, lower), weight_grad, chunks[last][0])
    return store_grad[None], weight_grad[None]


def solution(mesh):
    return jax.shard_map(
        per_device,
        mesh=mesh,
        in_specs=(
            P("pipe", None, "expert", None),
            P("pipe", None, None, None),
            P("pipe", None, None, "expert"),
            P("pipe", None, "expert"),
        ),
        out_specs=(P("pipe", None, None, "expert"), P("pipe", None, "expert")),
        check_vma=False,
    )
```
